32 devices in a mesh: member: 2 (over y), comp: 4 (over z), lev: 2 (over x), sub: 2 (over core).
Axes of the slice: x: 2, y: 2, z: 4, core: 2. Of those that a mesh axis runs over, the one named last changes fastest.
Arguments:
- atmos_state: float32 [4, 72, 8192], P(None, 'lev', ('member', 'comp', 'sub')), parts along dimension 2, may hold values from -6 to 6
- ocean_state: float32 [2, 80, 8192], P(None, None, ('member', 'comp', 'lev', 'sub')), parts along dimension 2, may hold values from -6 to 6
- level_weight: float32 [72], P('lev'), may hold values from 0.02 to 0.2
- atmos_neighbors: int32 [4, 4096], P(None, ('comp', 'sub')), may hold values from 0 to 639, as said below
- atmos_diffusion: float32 [4, 4096], P(None, ('comp', 'sub')), may hold values from 0.05 to 0.24
- ocean_neighbors: int32 [6, 4096], P(None, ('comp', 'lev', 'sub')), may hold values from 0 to 383, as said below
- ocean_diffusion: float32 [6, 4096], P(None, ('comp', 'lev', 'sub')), may hold values from 0.03 to 0.16
- vertical_mixing: float32 [4096], P(('comp', 'lev', 'sub')), may hold values from 0.05 to 0.45
- send_columns: int32 [4096], P(('comp', 'lev', 'sub')), may hold values from 0 to 511
- read_slots: int32 [4, 4096], P(None, ('comp', 'lev', 'sub')), may hold values from 0 to 255, as said below
- remap_weight: float32 [4, 4096], P(None, ('comp', 'lev', 'sub')), may hold values from 0.1 to 1
Outputs:
- atmos_out: float32 [4, 72, 8192], P(None, 'lev', ('member', 'comp', 'sub')), parts along dimension 2
- ocean_out: float32 [2, 80, 8192], P(None, None, ('member', 'comp', 'lev', 'sub')), parts along dimension 2
The draws below stay inside these ranges and needn't reach their ends.
There are 2 independent parts, one for each index of `member`. The reference program is written for one: setup_inputs(seed, part) draws one part's arguments, and reference() takes and returns one part's arrays. A program takes and returns all parts, laid end to end along the dimension named above; an argument that names none is the same for every part. Nothing has to cross between parts.
Inputs may be any that keep to these rules, and one draw needn't show every extreme that they name: `atmos_neighbors`: entry n of a column or cell in block b names place e of the block extended by 64 on each side: the neighbour is element 512 b + e - 64 of the whole, taken around the end. Every neighbour lies within 64 of the column. `ocean_neighbors`: as for the atmosphere, with blocks of 256 cells. `send_columns`: places 8 and up that a device fills for a position of its lev group are read only where that position is its own or adjacent to it, modulo 8. `read_slots`: A cell of a device at position d reads source position p = slot // 32 at place slot % 32; places of 8 and up only where p is d - 1, d or d + 1 modulo 8. Every place that may be read is read by some cell of the device.
All inputs are finite; a program needn't handle non-finite values.
Results may differ from the reference program's by a relative error of at most 0.0003.
Values sent between devices are 32-bit elements; how exact they have to be, the bound alone decides.
A program may use at most 64 MiB of HBM per device.

```python
import math
import jax
import jax.numpy as jnp
from jax import lax

FLDS = 4
ALEV = 72
OLEV = 80
NBA = 4
NBO = 6
KREM = 4
HALO = 64
STEPS_ATM = 4
STEPS_OCN = 2
ACOL = 512
OCELL = 256
HDEV = 8
GDEV = 16
CAPN = 32
CAPF = 8
ACOLS = 4096
OCELLS = 4096
N_COMP = 4
N_LEV = 2
N_SUB = 2


def local_links(key, links, cells, block, margin):
    size_key, sign_key = jax.random.split(key)
    magnitude = jax.random.randint(size_key, (links, cells), 1, margin + 1)
    direction = jax.random.randint(sign_key, (links, cells), 0, 2) * 2 - 1
    offsets = magnitude * direction
    place = jnp.arange(cells, dtype=jnp.int32) % block
    first_link = jnp.arange(links, dtype=jnp.int32)[:, None] == 0
    offsets = jnp.where(first_link & (place == 0), -margin, offsets)
    offsets = jnp.where(first_link & (place == block - 1), margin, offsets)
    return (place + margin + offsets).astype(jnp.int32)


def draw_atmos_neighbors(key, part):
    key = jax.random.fold_in(key, 11)
    return local_links(key, NBA, ACOLS, ACOL, HALO)


def draw_ocean_neighbors(key, part):
    key = jax.random.fold_in(key, 23)
    return local_links(key, NBO, OCELLS, OCELL, HALO)


def draw_read_slots(key, part):
    key = jax.random.fold_in(key, 37)
    live_count = 3 * CAPN + (HDEV - 3) * CAPF
    read_count = OCELL * KREM
    order = jnp.arange(live_count, dtype=jnp.int32)
    near_part = order < 3 * CAPN
    rank = jnp.where(near_part, order // CAPN, 3 + (order - 3 * CAPN) // CAPF)
    place = jnp.where(near_part, order % CAPN, (order - 3 * CAPN) % CAPF)

    def one_device(device):
        device_key = jax.random.fold_in(key, device)
        pick_key, shuffle_key = jax.random.split(device_key)
        position = device // (N_LEV * N_SUB) * N_SUB + device % N_SUB
        source = (position - 1 + rank) % HDEV
        live_slots = source * CAPN + place
        extra = jax.random.randint(pick_key, (read_count - live_count,), 0, live_count)
        chosen = jnp.concatenate([live_slots, live_slots[extra]])
        shuffled = jax.random.permutation(shuffle_key, chosen)
        return shuffled.reshape(OCELL, KREM).T
    per_device = jax.vmap(one_device)(jnp.arange(GDEV, dtype=jnp.int32))
    return per_device.transpose(1, 0, 2).reshape(KREM, OCELLS).astype(jnp.int32)


def touch_ends(drawn, rng, low, top_value):
    longest = drawn.shape.index(max(drawn.shape))
    spots = []
    for shift in (0, 1):
        where = [jax.random.randint(jax.random.fold_in(rng, axis), (), 0, length) for axis, length in enumerate(drawn.shape)]
        where[longest] = (where[longest] + shift) % drawn.shape[longest]
        spots.append(tuple(where))
    return drawn.at[spots[0]].set(low).at[spots[1]].set(top_value)


def block_levels(key, dims, shards, smallest, high):
    level = 1.0
    for axis_at, shards_of in shards:
        steps = jax.random.uniform(jax.random.fold_in(jax.random.fold_in(key, 6), axis_at), (shards_of,), jnp.float32, smallest / len(shards), high / len(shards))
        level = level * jnp.repeat(jnp.exp(steps), dims[axis_at] // shards_of).reshape((-1,) + (1,) * (len(dims) - 1 - axis_at))
    return level


def bell_draw(own_key, extent, deviation, reach, cuts=(), kind=jnp.bfloat16):
    result = jax.random.normal(own_key, extent, jnp.float32) * deviation
    if len(cuts) > 0:
        result = block_levels(own_key, extent, cuts, -0.22, 0.18) * result
    return jnp.clip(result, min=-reach, max=reach).astype(kind)


def setup_inputs(seed: int = 0, part: int = 0) -> dict:
    streams_of = jax.random.split(jax.random.key(seed), 12)
    part_keys = jax.random.split(jax.random.fold_in(streams_of[11], part), 12)
    atmos_state = bell_draw(part_keys[0], (FLDS, ALEV, ACOLS), 1.0, 6.0, ((1, 2), (2, 8)), jnp.float32)
    ocean_state = bell_draw(part_keys[1], (2, OLEV, OCELLS), 1.0, 6.0, ((2, 16),), jnp.float32)
    level_weight = jnp.clip(jnp.exp(math.log(0.2) - 2.3025851 * jax.random.uniform(streams_of[2], (ALEV,), jnp.float32) ** block_levels(streams_of[2], (ALEV,), ((0, 2),), -0.2, 0.2)), 0.02, 0.2)
    atmos_neighbors = draw_atmos_neighbors(jax.random.fold_in(streams_of[11], 71), part)
    atmos_diffusion = jnp.clip(jnp.exp(math.log(0.24) - 1.5686159 * jax.random.uniform(streams_of[4], (NBA, ACOLS), jnp.float32) ** block_levels(streams_of[4], (NBA, ACOLS), ((1, 8),), -0.2, 0.2)), 0.05, 0.24)
    ocean_neighbors = draw_ocean_neighbors(jax.random.fold_in(streams_of[11], 71), part)
    ocean_diffusion = jnp.clip(jnp.exp(math.log(0.16) - 1.6739764 * jax.random.uniform(streams_of[6], (NBO, OCELLS), jnp.float32) ** block_levels(streams_of[6], (NBO, OCELLS), ((1, 16),), -0.2, 0.2)), 0.03, 0.16)
    vertical_mixing = jnp.clip(jnp.exp(math.log(0.45) - 2.1972245 * jax.random.uniform(streams_of[7], (OCELLS,), jnp.float32) ** block_levels(streams_of[7], (OCELLS,), ((0, 16),), -0.2, 0.2)), 0.05, 0.45)
    send_columns = touch_ends(jax.random.randint(streams_of[8], (GDEV * HDEV * CAPN,), 0, ACOL), jax.random.fold_in(streams_of[8], 1), 0, ACOL - 1).astype(jnp.int32)
    read_slots = draw_read_slots(jax.random.fold_in(streams_of[11], 71), part)
    remap_weight = jnp.clip(jnp.exp(math.log(1.0) - 2.3025851 * jax.random.uniform(streams_of[10], (KREM, OCELLS), jnp.float32) ** block_levels(streams_of[10], (KREM, OCELLS), ((1, 16),), -0.2, 0.2)), 0.1, 1.0)
    return {"atmos_state": atmos_state, "ocean_state": ocean_state, "level_weight": level_weight, "atmos_neighbors": atmos_neighbors, "atmos_diffusion": atmos_diffusion, "ocean_neighbors": ocean_neighbors, "ocean_diffusion": ocean_diffusion, "vertical_mixing": vertical_mixing, "send_columns": send_columns, "read_slots": read_slots, "remap_weight": remap_weight}


def widen(field_data, margin):
    lower_rim = jnp.roll(field_data, 1, axis=2)[..., -margin:]
    upper_rim = jnp.roll(field_data, -1, axis=2)[..., :margin]
    return jnp.concatenate([lower_rim, field_data, upper_rim], axis=-1)

def graph_mix(field_data, padded, neighbors, diffusion):
    tendency = jnp.zeros_like(field_data)
    for column_slot in range(neighbors.shape[0]):
        places = jnp.broadcast_to(neighbors[column_slot], field_data.shape)
        picked = jnp.take_along_axis(padded, places, axis=-1)
        tendency = tendency + diffusion[column_slot] * (picked - field_data)
    return field_data + tendency

def vertical(sea_state, mixing):
    upper_level = jnp.concatenate([sea_state[:, :1], sea_state[:, :-1]], axis=1)
    lower_level = jnp.concatenate([sea_state[:, 1:], sea_state[:, -1:]], axis=1)
    return sea_state + mixing * (upper_level - 2.0 * sea_state + lower_level)

def force(sea_state, remapped):
    surface_temp = sea_state[0, 0]
    surface_salt = sea_state[1, 0]
    wind_speed = jnp.sqrt(remapped[2] * remapped[2] + remapped[3] * remapped[3] + 1.0)
    evaporation = 0.2 * wind_speed * (0.5 * jnp.exp(0.25 * surface_temp) - remapped[1])
    heat_flux = 0.3 * wind_speed * (remapped[0] - surface_temp) - 1.5 * evaporation
    salt_flux = 0.5 * evaporation * (1.0 + 0.2 * surface_salt)
    return sea_state.at[0, 0].add(heat_flux).at[1, 0].add(salt_flux)

def reference(atmos_state, ocean_state, level_weight, atmos_neighbors, atmos_diffusion, ocean_neighbors, ocean_diffusion, vertical_mixing, send_columns, read_slots, remap_weight):
    air_state = atmos_state.reshape(FLDS, ALEV, HDEV, ACOL)
    air_links = atmos_neighbors.reshape(NBA, HDEV, ACOL)
    air_rates = atmos_diffusion.reshape(NBA, HDEV, ACOL)
    for substep in range(STEPS_ATM):
        air_state = graph_mix(air_state, widen(air_state, HALO), air_links, air_rates)
    near_air = lax.optimization_barrier(jnp.sum(level_weight[None, :, None, None] * air_state, axis=1))
    tables = send_columns.reshape(N_COMP, N_LEV, N_SUB, HDEV, CAPN).transpose(1, 0, 2, 3, 4).reshape(N_LEV, HDEV, HDEV, CAPN)
    slot_rows = read_slots.reshape(KREM, GDEV, OCELL).transpose(1, 0, 2)
    weight_rows = remap_weight.reshape(KREM, GDEV, OCELL).transpose(1, 0, 2)
    sources = jnp.arange(HDEV, dtype=jnp.int32)[:, None]

    def remap_one(inputs):
        device, slots_here, weights_here = inputs
        level_group = device // N_SUB % N_LEV
        position = device // (N_LEV * N_SUB) * N_SUB + device % N_SUB
        send_table = tables[level_group, :, position, :]
        buffer = near_air[:, sources, send_table].reshape(FLDS, HDEV * CAPN)
        picked = buffer[:, slots_here]
        return lax.optimization_barrier(jnp.sum(weights_here * picked, axis=1)) / lax.optimization_barrier(jnp.sum(weights_here, axis=0))
    remapped = lax.map(remap_one, (jnp.arange(GDEV, dtype=jnp.int32), slot_rows, weight_rows))
    sea_state = force(ocean_state.reshape(2, OLEV, GDEV, OCELL), remapped.transpose(1, 0, 2))
    sea_links = ocean_neighbors.reshape(NBO, GDEV, OCELL)
    sea_rates = ocean_diffusion.reshape(NBO, GDEV, OCELL)
    mixing = vertical_mixing.reshape(GDEV, OCELL)
    for substep in range(STEPS_OCN):
        sea_state = vertical(graph_mix(sea_state, widen(sea_state, HALO), sea_links, sea_rates), mixing)
    return (air_state.reshape(FLDS, ALEV, ACOLS), sea_state.reshape(2, OLEV, OCELLS))
```

```python
import functools

import jax
import jax.numpy as jnp
from jax import lax
from jax.experimental import pallas as pl
from jax.experimental.pallas import tpu as pltpu
from jax.sharding import PartitionSpec as P

HALO = 64
STEPS_ATM = 4
STEPS_OCN = 2
LANE = 128
MESH = pl.DeviceIdType.MESH


def pick(x, lanes):
    return jnp.take_along_axis(x, lanes, axis=1, mode="promise_in_bounds")


def lane_of(shape):
    return lax.broadcasted_iota(jnp.int32, shape, 1)


def mix_tile(first, second, places, rates, keep):
    shape = first.shape
    own = jnp.where(
        lane_of(shape) < HALO,
        pltpu.roll(first, HALO, axis=1),
        pltpu.roll(second, HALO, axis=1),
    )
    acc = keep * own
    for n in range(places.shape[0]):
        place = jnp.broadcast_to(places[n : n + 1], shape)
        lanes = jnp.bitwise_and(place, LANE - 1)
        value = jnp.where(place < LANE, pick(first, lanes), pick(second, lanes))
        acc = acc + rates[n : n + 1] * value
    return acc


def kernel(
    npos,
    nlev,
    air_hbm,
    sea_hbm,
    weight_ref,
    anb_ref,
    adf_ref,
    onb_ref,
    odf_ref,
    vm_ref,
    send_ref,
    slot_ref,
    rw_ref,
    air_out,
    sea_out,
    x0,
    xa,
    xb,
    y0,
    ya,
    rbuf,
    qbuf,
    aplace,
    arate,
    oplace,
    orate,
    table,
    pout,
    pin,
    flux,
    loc_sem,
    avg_send,
    avg_recv,
    tab_send,
    tab_recv,
    air_send,
    air_recv,
    sea_send,
    sea_recv,
    q_send,
    q_recv,
    route_send,
    route_recv,
):
    c, l, s = lax.axis_index("comp"), lax.axis_index("lev"), lax.axis_index("sub")
    ncomp = npos // 2
    d = 2 * c + s
    flds, levs, block = air_hbm.shape
    rim = STEPS_ATM * HALO
    cells = sea_hbm.shape[2]
    orim = STEPS_OCN * HALO
    cap = send_ref.shape[1] // npos
    nba, nbo, krem = anb_ref.shape[0], onb_ref.shape[0], slot_ref.shape[0]

    def at(pos, lev):
        pos = lax.rem(pos + npos, npos)
        return {"comp": pos // 2, "lev": lax.rem(lev + nlev, nlev), "sub": lax.rem(pos, 2)}

    def sea_at(step):
        g = lax.rem((c * nlev + l) * 2 + s + step + 2 * ncomp * nlev, 2 * ncomp * nlev)
        return {"comp": g // (2 * nlev), "lev": lax.rem(g // 2, nlev), "sub": lax.rem(g, 2)}

    load_air = pltpu.make_async_copy(air_hbm, x0.at[:, :, rim : rim + block], loc_sem.at[0])
    load_sea = pltpu.make_async_copy(sea_hbm, y0.at[:, :, orim : orim + cells], loc_sem.at[1])
    load_air.start()
    load_sea.start()

    barrier = pltpu.get_barrier_semaphore()
    for k in range(1, npos):
        pl.semaphore_signal(barrier, inc=1, device_id=at(d + k, l), device_id_type=MESH)
    for j in range(1, nlev):
        for w in (-1, 0, 1):
            pl.semaphore_signal(barrier, inc=1, device_id=at(d + w, l + j), device_id_type=MESH)

    def offsets(ref):
        places = ref[...]
        return (places - HALO - lane_of(places.shape)).astype(jnp.float32)

    own = slice(rim, rim + block)
    rbuf[0, 4 : 4 + nba, own] = adf_ref[...]
    rbuf[0, 8 : 8 + nba, own] = offsets(anb_ref)
    rbuf[0, 12:16, own] = jnp.zeros((4, block), jnp.float32)
    sea_own = slice(orim, orim + cells)
    qbuf[0:nbo, sea_own] = offsets(onb_ref)
    qbuf[6 : 6 + nbo, sea_own] = odf_ref[...]
    qbuf[12:13, sea_own] = vm_ref[...]
    qbuf[13 : 13 + krem, sea_own] = slot_ref[...].astype(jnp.float32)
    qbuf[17 : 17 + krem, sea_own] = rw_ref[...]
    qbuf[21:24, sea_own] = jnp.zeros((3, cells), jnp.float32)
    table[0] = jnp.broadcast_to(send_ref[...], table.shape[1:])

    load_air.wait()
    weight = weight_ref[...]
    for f in range(flds):
        rbuf[0, f : f + 1, own] = jnp.sum(weight * x0[f, :, own], axis=0, keepdims=True)
    load_sea.wait()

    pl.semaphore_wait(barrier, npos - 1 + 3 * (nlev - 1))

    def remote(src, dst, send, recv, device):
        return pltpu.make_async_remote_copy(
            src_ref=src, dst_ref=dst, send_sem=send, recv_sem=recv,
            device_id=device, device_id_type=MESH,
        )

    copies = []
    avg = []
    lefts = slice(0, rim)
    rights = slice(rim + block, rim + block + rim)
    low = slice(rim, 2 * rim)
    high = slice(block, block + rim)
    for j in range(nlev):
        rel = (nlev - j) % nlev
        rows = slice(0, 16) if j == 0 else slice(0, 8)
        for w, (src, dst, step) in enumerate(((high, lefts, 1), (own, own, 0), (low, rights, -1))):
            if j == 0 and step == 0:
                continue
            avg.append(
                remote(
                    rbuf.at[0, rows, src], rbuf.at[rel, rows, dst],
                    avg_send.at[rel * 3 + w], avg_recv.at[rel * 3 + w], at(d + step, l + j),
                )
            )
    tabs = [remote(table.at[0], table.at[1], tab_send.at[0], tab_recv.at[0], at(d, l + 1))]
    if nlev > 2:
        tabs.append(remote(table.at[0], table.at[2], tab_send.at[1], tab_recv.at[1], at(d, l - 1)))
    q_high, q_left = slice(cells, cells + orim), slice(0, orim)
    q_low, q_right = slice(orim, 2 * orim), slice(orim + cells, orim + cells + orim)
    qs = [
        remote(qbuf.at[:, q_high], qbuf.at[:, q_left], q_send.at[0], q_recv.at[0], sea_at(1)),
        remote(qbuf.at[:, q_low], qbuf.at[:, q_right], q_send.at[1], q_recv.at[1], sea_at(-1)),
    ]
    seas = [
        remote(y0.at[:, :, q_high], y0.at[:, :, q_left], sea_send.at[0], sea_recv.at[0], sea_at(1)),
        remote(y0.at[:, :, q_low], y0.at[:, :, q_right], sea_send.at[1], sea_recv.at[1], sea_at(-1)),
    ]
    airs = [
        remote(x0.at[:, :, high], x0.at[:, :, lefts], air_send.at[0], air_recv.at[0], at(d + 1, l)),
        remote(x0.at[:, :, low], x0.at[:, :, rights], air_send.at[1], air_recv.at[1], at(d - 1, l)),
    ]
    for copy in avg + tabs + qs + seas + airs:
        copy.start()

    for copy in avg:
        copy.wait_recv()
    packed = rbuf[0]
    wide = packed.shape[1]
    for shift in range(2):
        moved = pltpu.roll(packed, wide - HALO, axis=1) if shift else packed
        rates = moved[4 : 4 + nba]
        tile_lane = jnp.bitwise_and(lane_of((nba, wide)), LANE - 1)
        aplace[shift, 0:nba] = moved[8 : 8 + nba].astype(jnp.int32) + tile_lane + HALO
        arate[shift, 0:nba] = rates
        arate[shift, nba : nba + 1] = 1.0 - jnp.sum(rates, axis=0, keepdims=True)

    def air_tile(k, t, first, second):
        shift, base = (1 - k % 2), (k + 1) // 2
        cols = slice((base + t) * LANE, (base + t + 1) * LANE)
        return mix_tile(
            first, second, aplace[shift, 0:nba, cols], arate[shift, 0:nba, cols],
            arate[shift, nba : nba + 1, cols],
        )

    total = rbuf[0, 0:8]
    for j in range(1, nlev):
        total = total + rbuf[j, 0:8]
    top = lax.broadcasted_iota(jnp.int32, (8, LANE), 0)
    tiles = []
    for t in range(wide // LANE):
        tile = total[:, t * LANE : (t + 1) * LANE]
        tiles.append(jnp.where(top < 4, tile, pltpu.roll(tile, 4, axis=0)))
    for k in range(STEPS_ATM):
        tiles = [air_tile(k, t, tiles[t], tiles[t + 1]) for t in range(len(tiles) - 1)]

    for copy in tabs:
        copy.wait_recv()
    lane8 = lane_of((8, LANE))
    per_tile = LANE // cap
    up_row = 2 if nlev > 2 else 1

    def request(pos):
        odd = lax.rem(pos, 2)
        forward = jnp.where(odd == 0, l > 0, l == nlev - 1)
        cross = lax.rem(pos + jnp.where(forward, 1, npos - 1), npos)
        start = pl.multiple_of(pos // per_tile * LANE, LANE)
        mine = table[0, :, pl.ds(start, LANE)]
        mine = pltpu.roll(mine, lax.rem(LANE - lax.rem(pos, per_tile) // 2 * 2 * cap, LANE), axis=1)
        start = pl.multiple_of(cross // per_tile * LANE, LANE)
        row = jnp.where(odd == 0, 1, up_row)
        other = table[row, :, pl.ds(start, LANE)]
        turn = lax.rem(2 * cap - lax.rem(cross, per_tile) * cap + LANE, LANE)
        other = pltpu.roll(other, turn, axis=1)
        column = jnp.where(lane8 < 2 * cap, mine, other)
        lanes = jnp.bitwise_and(column, LANE - 1)
        value = pick(tiles[0], lanes)
        for t in range(1, len(tiles)):
            value = jnp.where(column >= t * LANE, pick(tiles[t], lanes), value)
        return value

    routes = []
    for k in range(npos):
        pos = lax.rem(d + k, npos)
        if k == 0:
            pin[0] = request(pos)
            continue
        pout[k] = request(pos)
        copy = remote(pout.at[k], pin.at[k], route_send.at[k], route_recv.at[k], at(pos, l))
        copy.start()
        routes.append(copy)

    for copy in qs + seas:
        copy.wait_recv()
    qall = qbuf[...]
    qwide = qall.shape[1]
    for shift in range(2):
        moved = pltpu.roll(qall, qwide - HALO, axis=1) if shift else qall
        rates = moved[6 : 6 + nbo]
        tile_lane = jnp.bitwise_and(lane_of((nbo, qwide)), LANE - 1)
        oplace[shift, 0:nbo] = moved[0:nbo].astype(jnp.int32) + tile_lane + HALO
        orate[shift, 0:nbo] = rates
        orate[shift, nbo : nbo + 1] = 1.0 - jnp.sum(rates, axis=0, keepdims=True)
        orate[shift, nbo + 1 : nbo + 2] = moved[12:13]

    def sea_cols(k, t):
        base = (k + 1) // 2
        return 1 - k % 2, slice((base + t) * LANE, (base + t + 1) * LANE)

    def sea_tile(k, t, first, second):
        shift, cols = sea_cols(k, t)
        return mix_tile(
            first, second, oplace[shift, 0:nbo, cols], orate[shift, 0:nbo, cols],
            orate[shift, nbo : nbo + 1, cols],
        )

    def sea_vertical(k, t):
        shift, cols = sea_cols(k, t)
        return orate[shift, nbo + 1 : nbo + 2, cols]

    src = y0
    for k in range(STEPS_OCN):
        dst = sea_out if k == STEPS_OCN - 1 else ya

        def sea_step(tracer, carry, k=k, src=src, dst=dst):
            depth = src.shape[1]
            level = lax.broadcasted_iota(jnp.int32, (depth, LANE), 0)
            for t in range(dst.shape[2] // LANE):
                first = src[tracer, :, t * LANE : (t + 1) * LANE]
                second = src[tracer, :, (t + 1) * LANE : (t + 2) * LANE]
                v = sea_tile(k, t, first, second)
                up = jnp.where(level == 0, v, pltpu.roll(v, 1, axis=0))
                down = jnp.where(level == depth - 1, v, pltpu.roll(v, depth - 1, axis=0))
                v = v + sea_vertical(k, t) * (up - 2.0 * v + down)
                dst[tracer, :, t * LANE : (t + 1) * LANE] = v
            return carry

        lax.fori_loop(0, src.shape[0], sea_step, 0)
        src = dst

    for copy in airs:
        copy.wait_recv()
    src = x0
    for k in range(STEPS_ATM):
        dst = air_out if k == STEPS_ATM - 1 else (xa if k % 2 == 0 else xb)
        count = wide // LANE - 1 - k

        def air_step(f, carry, k=k, src=src, dst=dst, count=count):
            for t in range(count):
                first = src[f, :, t * LANE : (t + 1) * LANE]
                second = src[f, :, (t + 1) * LANE : (t + 2) * LANE]
                dst[f, :, t * LANE : (t + 1) * LANE] = air_tile(k, t, first, second)
            return carry

        lax.fori_loop(0, flds, air_step, 0)
        src = dst

    for copy in routes:
        copy.wait_recv()
    sub8 = lax.broadcasted_iota(jnp.int32, (8, LANE), 0)
    kinds = [jnp.where(s == 0, 2, 0)] + [s] * (cells // LANE) + [jnp.where(s == 0, 1, 2)]
    changes = []
    for t in range(qwide // LANE):
        cols = slice(t * LANE, (t + 1) * LANE)
        slots = qbuf[13 : 13 + krem, cols].astype(jnp.int32)
        weights = qbuf[17 : 17 + krem, cols]
        acc = jnp.zeros((8, LANE), jnp.float32)
        for m in range(krem // 2):
            m2 = m + krem // 2
            slot = jnp.where(sub8 < 4, slots[m : m + 1], slots[m2 : m2 + 1])
            weight2 = jnp.where(sub8 < 4, weights[m : m + 1], weights[m2 : m2 + 1])
            far = lax.rem(d - slot // cap + npos, npos)
            lanes = lax.rem(slot, cap) + kinds[t] * cap
            value = pick(pin[0], lanes)
            for k in range(1, npos):
                value = jnp.where(far == k, pick(pin[k], lanes), value)
            acc = acc + weight2 * value
        acc = acc + pltpu.roll(acc, 4, axis=0)
        acc = acc / jnp.sum(weights, axis=0, keepdims=True)
        temp, humid, east, north = (acc[i : i + 1] for i in range(4))
        sst = y0[0, 0:1, cols]
        salt = y0[1, 0:1, cols]
        wind = jnp.sqrt(east * east + north * north + 1.0)
        evap = 0.2 * wind * (0.5 * jnp.exp(0.25 * sst) - humid)
        heat = 0.3 * wind * (temp - sst) - 1.5 * evap
        brine = 0.5 * evap * (1.0 + 0.2 * salt)
        changes.append(jnp.where(sub8 == 0, heat, jnp.where(sub8 == 1, brine, 0.0)))
    later = []
    for t in range(len(changes) - 1):
        v = sea_tile(0, t, changes[t], changes[t + 1])
        mixing = sea_vertical(0, t)
        later.append(jnp.where(sub8 < 2, (1.0 - mixing) * v, mixing * pltpu.roll(v, 2, axis=0)))
    for t in range(len(later) - 1):
        v = sea_tile(1, t, later[t], later[t + 1])
        mixing = sea_vertical(1, t)
        cols = slice(t * LANE, (t + 1) * LANE)
        for tracer in range(2):
            a, b = v[tracer : tracer + 1], v[2 + tracer : 3 + tracer]
            sea_out[tracer, 0:1, cols] += a + mixing * (b - a)
            sea_out[tracer, 1:2, cols] += b + mixing * (a - 2.0 * b)
            sea_out[tracer, 2:3, cols] += mixing * b

    for copy in avg + tabs + qs + seas + airs + routes:
        copy.wait_send()


def body(
    npos,
    nlev,
    atmos_state,
    ocean_state,
    level_weight,
    atmos_neighbors,
    atmos_diffusion,
    ocean_neighbors,
    ocean_diffusion,
    vertical_mixing,
    send_columns,
    read_slots,
    remap_weight,
):
    flds, levs, block = atmos_state.shape
    tracers, depth, cells = ocean_state.shape
    wide = block + 2 * STEPS_ATM * HALO
    qwide = cells + 2 * STEPS_OCN * HALO
    vmem = pl.BlockSpec(memory_space=pltpu.VMEM)
    anywhere = pl.BlockSpec(memory_space=pl.ANY)
    dma = pltpu.SemaphoreType.DMA
    places = send_columns.shape[0]
    return pl.pallas_call(
        functools.partial(kernel, npos, nlev),
        out_shape=(
            jax.ShapeDtypeStruct(atmos_state.shape, jnp.float32),
            jax.ShapeDtypeStruct(ocean_state.shape, jnp.float32),
        ),
        in_specs=[anywhere] * 2 + [vmem] * 9,
        out_specs=(vmem, vmem),
        scratch_shapes=[
            pltpu.VMEM((flds, levs, wide), jnp.float32),
            pltpu.VMEM((flds, levs, wide - LANE), jnp.float32),
            pltpu.VMEM((flds, levs, wide - 2 * LANE), jnp.float32),
            pltpu.VMEM((tracers, depth, qwide), jnp.float32),
            pltpu.VMEM((tracers, depth, qwide - LANE), jnp.float32),
            pltpu.VMEM((nlev, 16, wide), jnp.float32),
            pltpu.VMEM((24, qwide), jnp.float32),
            pltpu.VMEM((2, 8, wide), jnp.int32),
            pltpu.VMEM((2, 8, wide), jnp.float32),
            pltpu.VMEM((2, 8, qwide), jnp.int32),
            pltpu.VMEM((2, 8, qwide), jnp.float32),
            pltpu.VMEM((3, 8, places), jnp.int32),
            pltpu.VMEM((npos, 8, LANE), jnp.float32),
            pltpu.VMEM((npos, 8, LANE), jnp.float32),
            pltpu.VMEM((8, LANE), jnp.float32),
            dma((2,)),
            dma((3 * nlev,)),
            dma((3 * nlev,)),
            dma((2,)),
            dma((2,)),
            dma((2,)),
            dma((2,)),
            dma((2,)),
            dma((2,)),
            dma((2,)),
            dma((2,)),
            dma((npos,)),
            dma((npos,)),
        ],
        compiler_params=pltpu.CompilerParams(
            collective_id=0, has_side_effects=True, vmem_limit_bytes=32 * 1024 * 1024
        ),
    )(
        atmos_state,
        ocean_state,
        level_weight[:, None],
        atmos_neighbors,
        atmos_diffusion,
        ocean_neighbors,
        ocean_diffusion,
        vertical_mixing[None, :],
        send_columns[None, :],
        read_slots,
        remap_weight,
    )


def solution(mesh):
    npos = mesh.shape["comp"] * mesh.shape["sub"]
    nlev = mesh.shape["lev"]
    in_specs = (
        P(None, "lev", ("member", "comp", "sub")),
        P(None, None, ("member", "comp", "lev", "sub")),
        P("lev"),
        P(None, ("comp", "sub")),
        P(None, ("comp", "sub")),
        P(None, ("comp", "lev", "sub")),
        P(None, ("comp", "lev", "sub")),
        P(("comp", "lev", "sub")),
        P(("comp", "lev", "sub")),
        P(None, ("comp", "lev", "sub")),
        P(None, ("comp", "lev", "sub")),
    )
    out_specs = (
        P(None, "lev", ("member", "comp", "sub")),
        P(None, None, ("member", "comp", "lev", "sub")),
    )
    return jax.shard_map(
        functools.partial(body, npos, nlev),
        mesh=mesh,
        in_specs=in_specs,
        out_specs=out_specs,
        check_vma=False,
    )
```

```python
import functools

import jax
import jax.numpy as jnp
from jax import lax
from jax.experimental import pallas as pl
from jax.experimental.pallas import tpu as pltpu
from jax.sharding import PartitionSpec as P

HALO = 64
STEPS_ATM = 4
STEPS_OCN = 2
LANE = 128
MESH = pl.DeviceIdType.MESH


def pick(x, lanes):
    return jnp.take_along_axis(x, lanes, axis=1, mode="promise_in_bounds")


def lane_of(shape):
    return lax.broadcasted_iota(jnp.int32, shape, 1)


def mix_tile(first, second, places, rates, keep):
    shape = first.shape
    own = jnp.where(
        lane_of(shape) < HALO,
        pltpu.roll(first, HALO, axis=1),
        pltpu.roll(second, HALO, axis=1),
    )
    acc = keep * own
    for n in range(places.shape[0]):
        place = jnp.broadcast_to(places[n : n + 1], shape)
        lanes = jnp.bitwise_and(place, LANE - 1)
        value = jnp.where(place < LANE, pick(first, lanes), pick(second, lanes))
        acc = acc + rates[n : n + 1] * value
    return acc


def kernel(
    npos,
    nlev,
    air_hbm,
    sea_hbm,
    weight_hbm,
    *rest,
):
    (
    anb_hbm,
    adf_hbm,
    onb_hbm,
    odf_hbm,
    vm_hbm,
    send_hbm,
    slot_hbm,
    rw_hbm,
    air_out,
    sea_out,
    weight_ref,
    anb_ref,
    adf_ref,
    onb_ref,
    odf_ref,
    vm_ref,
    send_ref,
    slot_ref,
    rw_ref,
    x0,
    xf,
    xa,
    xb,
    mats,
    y0,
    ya,
    rbuf,
    qbuf,
    aplace,
    arate,
    oplace,
    orate,
    table,
    pout,
    pin,
    loc_sem,
    avg_send,
    avg_recv,
    tab_send,
    tab_recv,
    air_send,
    air_recv,
    sea_send,
    sea_recv,
    q_send,
    q_recv,
    route_send,
    route_recv,
    ) = rest
    c, l, s = lax.axis_index("comp"), lax.axis_index("lev"), lax.axis_index("sub")
    ncomp = npos // 2
    d = 2 * c + s
    levs, flds, block = air_hbm.shape
    rim = STEPS_ATM * HALO
    cells = sea_hbm.shape[2]
    orim = STEPS_OCN * HALO
    cap = send_ref.shape[1] // npos
    nba, nbo, krem = anb_ref.shape[0], onb_ref.shape[0], slot_ref.shape[0]

    def at(pos, lev):
        pos = lax.rem(pos + npos, npos)
        return {"comp": pos // 2, "lev": lax.rem(lev + nlev, nlev), "sub": lax.rem(pos, 2)}

    def sea_at(step):
        g = lax.rem((c * nlev + l) * 2 + s + step + 2 * ncomp * nlev, 2 * ncomp * nlev)
        return {"comp": g // (2 * nlev), "lev": lax.rem(g // 2, nlev), "sub": lax.rem(g, 2)}

    barrier = pltpu.get_barrier_semaphore()
    for k in range(1, npos):
        pl.semaphore_signal(barrier, inc=1, device_id=at(d + k, l), device_id_type=MESH)
    for j in range(1, nlev):
        for w in (-1, 0, 1):
            pl.semaphore_signal(barrier, inc=1, device_id=at(d + w, l + j), device_id_type=MESH)

    load_air = pltpu.make_async_copy(air_hbm, x0.at[:, :, rim : rim + block], loc_sem.at[0])
    load_sea = pltpu.make_async_copy(sea_hbm, y0.at[:, :, orim : orim + cells], loc_sem.at[1])
    small = [
        pltpu.make_async_copy(src, dst, loc_sem.at[2 + i])
        for i, (src, dst) in enumerate((
            (weight_hbm, weight_ref), (anb_hbm, anb_ref), (adf_hbm, adf_ref),
            (send_hbm, send_ref), (onb_hbm, onb_ref), (odf_hbm, odf_ref), (vm_hbm, vm_ref),
            (slot_hbm, slot_ref), (rw_hbm, rw_ref),
        ))
    ]
    load_air.start()
    for copy in small:
        copy.start()
    load_sea.start()
    for copy in small:
        copy.wait()

    def offsets(ref):
        places = ref[...]
        return (places - HALO - lane_of(places.shape)).astype(jnp.float32)

    own = slice(rim, rim + block)
    rbuf[0, 4 : 4 + nba, own] = adf_ref[...]
    rbuf[0, 8 : 8 + nba, own] = offsets(anb_ref)
    rbuf[0, 12:16, own] = jnp.zeros((4, block), jnp.float32)
    sea_own = slice(orim, orim + cells)
    qbuf[0:nbo, sea_own] = offsets(onb_ref)
    qbuf[6 : 6 + nbo, sea_own] = odf_ref[...]
    qbuf[12:13, sea_own] = vm_ref[...]
    qbuf[13 : 13 + krem, sea_own] = slot_ref[...].astype(jnp.float32)
    qbuf[17 : 17 + krem, sea_own] = rw_ref[...]
    qbuf[21:24, sea_own] = jnp.zeros((3, cells), jnp.float32)
    table[0] = jnp.broadcast_to(send_ref[...], table.shape[1:])

    load_air.wait()
    sums = [weight_ref[k] * x0[k, :, own] for k in range(4)]
    for k in range(4, levs):
        sums[k % 4] = sums[k % 4] + weight_ref[k] * x0[k, :, own]
    rbuf[0, 0:flds, own] = (sums[0] + sums[1]) + (sums[2] + sums[3])
    load_sea.wait()

    pl.semaphore_wait(barrier, npos - 1 + 3 * (nlev - 1))

    def remote(src, dst, send, recv, device):
        return pltpu.make_async_remote_copy(
            src_ref=src, dst_ref=dst, send_sem=send, recv_sem=recv,
            device_id=device, device_id_type=MESH,
        )

    copies = []
    avg = []
    lefts = slice(0, rim)
    rights = slice(rim + block, rim + block + rim)
    low = slice(rim, 2 * rim)
    high = slice(block, block + rim)
    for j in range(nlev):
        rel = (nlev - j) % nlev
        rows = slice(0, 16) if j == 0 else slice(0, 8)
        for w, (src, dst, step) in enumerate(((high, lefts, 1), (own, own, 0), (low, rights, -1))):
            if j == 0 and step == 0:
                continue
            avg.append(
                remote(
                    rbuf.at[0, rows, src], rbuf.at[rel, rows, dst],
                    avg_send.at[rel * 3 + w], avg_recv.at[rel * 3 + w], at(d + step, l + j),
                )
            )
    tabs = [remote(table.at[0], table.at[1], tab_send.at[0], tab_recv.at[0], at(d, l + 1))]
    if nlev > 2:
        tabs.append(remote(table.at[0], table.at[2], tab_send.at[1], tab_recv.at[1], at(d, l - 1)))
    q_high, q_left = slice(cells, cells + orim), slice(0, orim)
    q_low, q_right = slice(orim, 2 * orim), slice(orim + cells, orim + cells + orim)
    qs = [
        remote(qbuf.at[:, q_high], qbuf.at[:, q_left], q_send.at[0], q_recv.at[0], sea_at(1)),
        remote(qbuf.at[:, q_low], qbuf.at[:, q_right], q_send.at[1], q_recv.at[1], sea_at(-1)),
    ]
    seas = [
        remote(y0.at[:, :, q_high], y0.at[:, :, q_left], sea_send.at[0], sea_recv.at[0], sea_at(1)),
        remote(y0.at[:, :, q_low], y0.at[:, :, q_right], sea_send.at[1], sea_recv.at[1], sea_at(-1)),
    ]
    airs = [
        remote(x0.at[:, :, high], x0.at[:, :, lefts], air_send.at[0], air_recv.at[0], at(d + 1, l)),
        remote(x0.at[:, :, low], x0.at[:, :, rights], air_send.at[1], air_recv.at[1], at(d - 1, l)),
    ]
    for copy in avg + tabs + qs + seas + airs:
        copy.start()

    def tables(data, shift):
        span = data.shape[1]
        moved = pltpu.roll(data, span - HALO, axis=1) if shift else data
        rates = moved[4 : 4 + nba]
        tile_lane = jnp.bitwise_and(lane_of((nba, span)), LANE - 1)
        places = moved[8 : 8 + nba].astype(jnp.int32) + tile_lane + HALO
        return places, rates, 1.0 - jnp.sum(rates, axis=0, keepdims=True)

    row_ids = lax.broadcasted_iota(jnp.int32, (2 * LANE, LANE), 0)
    self_ids = lane_of((2 * LANE, LANE)) + HALO

    def build(index, places, rates, keep):
        matrix = jnp.where(row_ids == self_ids, keep, 0.0)
        for n in range(nba):
            matrix = matrix + jnp.where(row_ids == places[n : n + 1], rates[n : n + 1], 0.0)
        upper = matrix.astype(jnp.bfloat16)
        mats[index, :, 0:LANE] = upper
        mats[index, :, LANE:] = (matrix - upper.astype(jnp.float32)).astype(jnp.bfloat16)

    wide = rbuf.shape[2]
    own_data = rbuf[0, :, own]
    rim_tiles, block_tiles = rim // LANE, block // LANE
    shifted_count = wide // LANE - 1
    done = set()
    for shift in range(2):
        places, rates, keep = tables(own_data, shift)
        for t in range(block_tiles - shift):
            cols = slice(t * LANE, (t + 1) * LANE)
            index = rim_tiles + t + (0 if shift else shifted_count - 1)
            build(index, places[:, cols], rates[:, cols], keep[:, cols])
            done.add(index)

    def flatten(cols):
        for k in range(0, levs, 2):
            xf[4 * k : 4 * k + 8, cols] = jnp.concatenate([x0[k, :, cols], x0[k + 1, :, cols]], axis=0)

    flatten(own)

    for copy in avg:
        copy.wait_recv()
    packed = rbuf[0]
    for shift in range(2):
        places, rates, keep = tables(packed, shift)
        aplace[shift, 0:nba] = places
        arate[shift, 0:nba] = rates
        arate[shift, nba : nba + 1] = keep

    def air_tile(k, t, first, second):
        shift, base = (1 - k % 2), (k + 1) // 2
        cols = slice((base + t) * LANE, (base + t + 1) * LANE)
        return mix_tile(
            first, second, aplace[shift, 0:nba, cols], arate[shift, 0:nba, cols],
            arate[shift, nba : nba + 1, cols],
        )

    total = rbuf[0, 0:8]
    for j in range(1, nlev):
        total = total + rbuf[j, 0:8]
    top = lax.broadcasted_iota(jnp.int32, (8, LANE), 0)
    tiles = []
    for t in range(wide // LANE):
        tile = total[:, t * LANE : (t + 1) * LANE]
        tiles.append(jnp.where(top < 4, tile, pltpu.roll(tile, 4, axis=0)))
    for k in range(STEPS_ATM):
        tiles = [air_tile(k, t, tiles[t], tiles[t + 1]) for t in range(len(tiles) - 1)]

    for copy in tabs:
        copy.wait_recv()
    lane8 = lane_of((8, LANE))
    per_tile = LANE // cap
    up_row = 2 if nlev > 2 else 1

    def request(pos):
        odd = lax.rem(pos, 2)
        forward = jnp.where(odd == 0, l > 0, l == nlev - 1)
        cross = lax.rem(pos + jnp.where(forward, 1, npos - 1), npos)
        start = pl.multiple_of(pos // per_tile * LANE, LANE)
        mine = table[0, :, pl.ds(start, LANE)]
        mine = pltpu.roll(mine, lax.rem(LANE - lax.rem(pos, per_tile) // 2 * 2 * cap, LANE), axis=1)
        start = pl.multiple_of(cross // per_tile * LANE, LANE)
        row = jnp.where(odd == 0, 1, up_row)
        other = table[row, :, pl.ds(start, LANE)]
        turn = lax.rem(2 * cap - lax.rem(cross, per_tile) * cap + LANE, LANE)
        other = pltpu.roll(other, turn, axis=1)
        column = jnp.where(lane8 < 2 * cap, mine, other)
        lanes = jnp.bitwise_and(column, LANE - 1)
        value = pick(tiles[0], lanes)
        for t in range(1, len(tiles)):
            value = jnp.where(column >= t * LANE, pick(tiles[t], lanes), value)
        return value

    routes = []
    for k in range(npos):
        pos = lax.rem(d + k, npos)
        if k == 0:
            pin[0] = request(pos)
            continue
        pout[k] = request(pos)
        copy = remote(pout.at[k], pin.at[k], route_send.at[k], route_recv.at[k], at(pos, l))
        copy.start()
        routes.append(copy)

    for copy in qs + seas:
        copy.wait_recv()
    qall = qbuf[...]
    qwide = qall.shape[1]
    for shift in range(2):
        moved = pltpu.roll(qall, qwide - HALO, axis=1) if shift else qall
        rates = moved[6 : 6 + nbo]
        tile_lane = jnp.bitwise_and(lane_of((nbo, qwide)), LANE - 1)
        oplace[shift, 0:nbo] = moved[0:nbo].astype(jnp.int32) + tile_lane + HALO
        orate[shift, 0:nbo] = rates
        orate[shift, nbo : nbo + 1] = 1.0 - jnp.sum(rates, axis=0, keepdims=True)
        orate[shift, nbo + 1 : nbo + 2] = moved[12:13]

    def sea_cols(k, t):
        base = (k + 1) // 2
        return 1 - k % 2, slice((base + t) * LANE, (base + t + 1) * LANE)

    def sea_tile(k, t, first, second):
        shift, cols = sea_cols(k, t)
        return mix_tile(
            first, second, oplace[shift, 0:nbo, cols], orate[shift, 0:nbo, cols],
            orate[shift, nbo : nbo + 1, cols],
        )

    def sea_vertical(k, t):
        shift, cols = sea_cols(k, t)
        return orate[shift, nbo + 1 : nbo + 2, cols]

    src = y0
    for k in range(STEPS_OCN):
        dst = sea_out if k == STEPS_OCN - 1 else ya

        def sea_step(tracer, carry, k=k, src=src, dst=dst):
            depth = src.shape[1]
            level = lax.broadcasted_iota(jnp.int32, (depth, LANE), 0)
            for t in range(dst.shape[2] // LANE):
                first = src[tracer, :, t * LANE : (t + 1) * LANE]
                second = src[tracer, :, (t + 1) * LANE : (t + 2) * LANE]
                v = sea_tile(k, t, first, second)
                up = jnp.where(level == 0, v, pltpu.roll(v, 1, axis=0))
                down = jnp.where(level == depth - 1, v, pltpu.roll(v, depth - 1, axis=0))
                v = v + sea_vertical(k, t) * (up - 2.0 * v + down)
                dst[tracer, :, t * LANE : (t + 1) * LANE] = v
            return carry

        lax.fori_loop(0, src.shape[0], sea_step, 0)
        src = dst

    for shift in range(2):
        for t in range(1 - shift, shifted_count):
            index = t + (0 if shift else shifted_count - 1)
            if index in done:
                continue
            cols = slice(t * LANE, (t + 1) * LANE)
            build(
                index, aplace[shift, 0:nba, cols], arate[shift, 0:nba, cols],
                arate[shift, nba : nba + 1, cols],
            )
    for copy in airs:
        copy.wait_recv()
    flatten(lefts)
    flatten(rights)
    rows = xf.shape[0]
    src = xf
    for k in range(STEPS_ATM):
        dst = xa if k % 2 == 0 else xb
        for t in range(shifted_count - k):
            shift, base = 1 - k % 2, (k + 1) // 2
            index = base + t + (0 if shift else shifted_count - 1)
            x = src[:, t * LANE : (t + 2) * LANE]
            upper = x.astype(jnp.bfloat16)
            lower = (x - upper.astype(jnp.float32)).astype(jnp.bfloat16)
            both = jnp.concatenate([upper, lower], axis=0)
            prod = jnp.dot(both, mats[index], preferred_element_type=jnp.float32)
            small_part = prod[rows:, 0:LANE] + prod[:rows, LANE:] + prod[rows:, LANE:]
            result = prod[:rows, 0:LANE] + small_part
            cols = slice(t * LANE, (t + 1) * LANE)
            if k < STEPS_ATM - 1:
                dst[:, cols] = result
            else:
                for level in range(levs):
                    air_out[level, :, cols] = result[4 * level : 4 * level + 4]
        src = dst

    for copy in routes:
        copy.wait_recv()
    sub8 = lax.broadcasted_iota(jnp.int32, (8, LANE), 0)
    kinds = [jnp.where(s == 0, 2, 0)] + [s] * (cells // LANE) + [jnp.where(s == 0, 1, 2)]
    changes = []
    for t in range(qwide // LANE):
        cols = slice(t * LANE, (t + 1) * LANE)
        slots = qbuf[13 : 13 + krem, cols].astype(jnp.int32)
        weights = qbuf[17 : 17 + krem, cols]
        acc = jnp.zeros((8, LANE), jnp.float32)
        for m in range(krem // 2):
            m2 = m + krem // 2
            slot = jnp.where(sub8 < 4, slots[m : m + 1], slots[m2 : m2 + 1])
            weight2 = jnp.where(sub8 < 4, weights[m : m + 1], weights[m2 : m2 + 1])
            far = lax.rem(d - slot // cap + npos, npos)
            lanes = lax.rem(slot, cap) + kinds[t] * cap
            value = pick(pin[0], lanes)
            for k in range(1, npos):
                value = jnp.where(far == k, pick(pin[k], lanes), value)
            acc = acc + weight2 * value
        acc = acc + pltpu.roll(acc, 4, axis=0)
        acc = acc / jnp.sum(weights, axis=0, keepdims=True)
        temp, humid, east, north = (acc[i : i + 1] for i in range(4))
        sst = y0[0, 0:1, cols]
        salt = y0[1, 0:1, cols]
        wind = jnp.sqrt(east * east + north * north + 1.0)
        evap = 0.2 * wind * (0.5 * jnp.exp(0.25 * sst) - humid)
        heat = 0.3 * wind * (temp - sst) - 1.5 * evap
        brine = 0.5 * evap * (1.0 + 0.2 * salt)
        changes.append(jnp.where(sub8 == 0, heat, jnp.where(sub8 == 1, brine, 0.0)))
    later = []
    for t in range(len(changes) - 1):
        v = sea_tile(0, t, changes[t], changes[t + 1])
        mixing = sea_vertical(0, t)
        later.append(jnp.where(sub8 < 2, (1.0 - mixing) * v, mixing * pltpu.roll(v, 2, axis=0)))
    for t in range(len(later) - 1):
        v = sea_tile(1, t, later[t], later[t + 1])
        mixing = sea_vertical(1, t)
        cols = slice(t * LANE, (t + 1) * LANE)
        for tracer in range(2):
            a, b = v[tracer : tracer + 1], v[2 + tracer : 3 + tracer]
            sea_out[tracer, 0:1, cols] += a + mixing * (b - a)
            sea_out[tracer, 1:2, cols] += b + mixing * (a - 2.0 * b)
            sea_out[tracer, 2:3, cols] += mixing * b

    for copy in avg + tabs + qs + seas + airs + routes:
        copy.wait_send()


def body(
    npos,
    nlev,
    atmos_state,
    ocean_state,
    level_weight,
    atmos_neighbors,
    atmos_diffusion,
    ocean_neighbors,
    ocean_diffusion,
    vertical_mixing,
    send_columns,
    read_slots,
    remap_weight,
):
    flds, levs, block = atmos_state.shape
    tracers, depth, cells = ocean_state.shape
    wide = block + 2 * STEPS_ATM * HALO
    qwide = cells + 2 * STEPS_OCN * HALO
    rows = -(-flds * levs // 16) * 16
    vmem = pl.BlockSpec(memory_space=pltpu.VMEM)
    hbm = pl.BlockSpec(memory_space=pltpu.HBM)
    dma = pltpu.SemaphoreType.DMA
    f32, i32 = jnp.float32, jnp.int32
    places = send_columns.shape[0]
    small = (
        (atmos_neighbors.shape, i32),
        (atmos_diffusion.shape, f32),
        (ocean_neighbors.shape, i32),
        (ocean_diffusion.shape, f32),
        ((1, cells), f32),
        ((1, places), i32),
        (read_slots.shape, i32),
        (remap_weight.shape, f32),
    )
    air, sea = pl.pallas_call(
        functools.partial(kernel, npos, nlev),
        out_shape=(
            jax.ShapeDtypeStruct((levs, flds, block), f32),
            jax.ShapeDtypeStruct(ocean_state.shape, f32),
        ),
        in_specs=[hbm] * 11,
        out_specs=(vmem, vmem),
        scratch_shapes=[
            pltpu.SMEM(level_weight.shape, f32),
            *(pltpu.VMEM(shape, kind) for shape, kind in small),
            pltpu.VMEM((levs, flds, wide), f32),
            pltpu.VMEM((rows, wide), f32),
            pltpu.VMEM((rows, wide - LANE), f32),
            pltpu.VMEM((rows, wide - 2 * LANE), f32),
            pltpu.VMEM((2 * wide // LANE - 3, 2 * LANE, 2 * LANE), jnp.bfloat16),
            pltpu.VMEM((tracers, depth, qwide), f32),
            pltpu.VMEM((tracers, depth, qwide - LANE), f32),
            pltpu.VMEM((nlev, 16, wide), f32),
            pltpu.VMEM((24, qwide), f32),
            pltpu.VMEM((2, 8, wide), i32),
            pltpu.VMEM((2, 8, wide), f32),
            pltpu.VMEM((2, 8, qwide), i32),
            pltpu.VMEM((2, 8, qwide), f32),
            pltpu.VMEM((3, 8, places), i32),
            pltpu.VMEM((npos, 8, LANE), f32),
            pltpu.VMEM((npos, 8, LANE), f32),
            dma((11,)),
            dma((3 * nlev,)),
            dma((3 * nlev,)),
            *(dma((2,)) for _ in range(8)),
            dma((npos,)),
            dma((npos,)),
        ],
        compiler_params=pltpu.CompilerParams(
            collective_id=0, has_side_effects=True, vmem_limit_bytes=32 * 1024 * 1024
        ),
    )(
        jnp.transpose(atmos_state, (1, 0, 2)),
        ocean_state,
        level_weight,
        atmos_neighbors,
        atmos_diffusion,
        ocean_neighbors,
        ocean_diffusion,
        vertical_mixing[None, :],
        send_columns[None, :],
        read_slots,
        remap_weight,
    )
    air, sea = pl.pallas_call(
        move_out,
        out_shape=(
            jax.ShapeDtypeStruct((levs, flds, block), f32),
            jax.ShapeDtypeStruct(ocean_state.shape, f32),
        ),
        in_specs=[vmem] * 2,
        out_specs=(hbm, hbm),
        scratch_shapes=[dma((2,))],
    )(air, sea)
    return jnp.transpose(air, (1, 0, 2)), sea


def move_out(air, sea, air_out, sea_out, sems):
    copies = [
        pltpu.make_async_copy(air, air_out, sems.at[0]),
        pltpu.make_async_copy(sea, sea_out, sems.at[1]),
    ]
    for copy in copies:
        copy.start()
    for copy in copies:
        copy.wait()


def solution(mesh):
    npos = mesh.shape["comp"] * mesh.shape["sub"]
    nlev = mesh.shape["lev"]
    in_specs = (
        P(None, "lev", ("member", "comp", "sub")),
        P(None, None, ("member", "comp", "lev", "sub")),
        P("lev"),
        P(None, ("comp", "sub")),
        P(None, ("comp", "sub")),
        P(None, ("comp", "lev", "sub")),
        P(None, ("comp", "lev", "sub")),
        P(("comp", "lev", "sub")),
        P(("comp", "lev", "sub")),
        P(None, ("comp", "lev", "sub")),
        P(None, ("comp", "lev", "sub")),
    )
    out_specs = (
        P(None, "lev", ("member", "comp", "sub")),
        P(None, None, ("member", "comp", "lev", "sub")),
    )
    return jax.shard_map(
        functools.partial(body, npos, nlev),
        mesh=mesh,
        in_specs=in_specs,
        out_specs=out_specs,
        check_vma=False,
    )
```

```python
import functools

import jax
import jax.numpy as jnp
from jax import lax
from jax.experimental import pallas as pl
from jax.experimental.pallas import tpu as pltpu
from jax.sharding import PartitionSpec as P

HALO = 64
STEPS_ATM = 4
STEPS_OCN = 2
LANE = 128
MESH = pl.DeviceIdType.MESH


def pick(x, lanes):
    return jnp.take_along_axis(x, lanes, axis=1, mode="promise_in_bounds")


def lane_of(shape):
    return lax.broadcasted_iota(jnp.int32, shape, 1)


def mix_tile(first, second, places, rates, keep):
    shape = first.shape
    own = jnp.where(
        lane_of(shape) < HALO,
        pltpu.roll(first, HALO, axis=1),
        pltpu.roll(second, HALO, axis=1),
    )
    acc = keep * own
    for n in range(places.shape[0]):
        place = jnp.broadcast_to(places[n : n + 1], shape)
        lanes = jnp.bitwise_and(place, LANE - 1)
        value = jnp.where(place < LANE, pick(first, lanes), pick(second, lanes))
        acc = acc + rates[n : n + 1] * value
    return acc


def kernel(
    npos,
    nlev,
    air_hbm,
    sea_hbm,
    weight_hbm,
    *rest,
):
    (
    anb_hbm,
    adf_hbm,
    onb_hbm,
    odf_hbm,
    vm_hbm,
    send_hbm,
    slot_hbm,
    rw_hbm,
    air_res,
    sea_res,
    air_out,
    sea_out,
    weight_ref,
    anb_ref,
    adf_ref,
    onb_ref,
    odf_ref,
    vm_ref,
    send_ref,
    slot_ref,
    rw_ref,
    x0,
    xf,
    xa,
    xb,
    mats,
    sea_mats,
    y0,
    ya,
    rbuf,
    qbuf,
    aplace,
    arate,
    oplace,
    orate,
    table,
    pout,
    pin,
    loc_sem,
    air_sem,
    out_sem,
    avg_send,
    avg_recv,
    tab_send,
    tab_recv,
    air_send,
    air_recv,
    sea_send,
    sea_recv,
    q_send,
    q_recv,
    route_send,
    route_recv,
    ) = rest
    c, l, s = lax.axis_index("comp"), lax.axis_index("lev"), lax.axis_index("sub")
    ncomp = npos // 2
    d = 2 * c + s
    levs, flds, block = air_hbm.shape
    rim = STEPS_ATM * HALO
    cells = sea_hbm.shape[2]
    orim = STEPS_OCN * HALO
    cap = send_ref.shape[1] // npos
    nba, nbo, krem = anb_ref.shape[0], onb_ref.shape[0], slot_ref.shape[0]

    def at(pos, lev):
        pos = lax.rem(pos + npos, npos)
        return {"comp": pos // 2, "lev": lax.rem(lev + nlev, nlev), "sub": lax.rem(pos, 2)}

    def sea_at(step):
        g = lax.rem((c * nlev + l) * 2 + s + step + 2 * ncomp * nlev, 2 * ncomp * nlev)
        return {"comp": g // (2 * nlev), "lev": lax.rem(g // 2, nlev), "sub": lax.rem(g, 2)}

    barrier = pltpu.get_barrier_semaphore()
    for k in range(1, npos):
        pl.semaphore_signal(barrier, inc=1, device_id=at(d + k, l), device_id_type=MESH)
    for j in range(1, nlev):
        for w in (-1, 0, 1):
            pl.semaphore_signal(barrier, inc=1, device_id=at(d + w, l + j), device_id_type=MESH)

    parts = parts_of(levs)
    chunk = levs // parts
    load_air = [
        pltpu.make_async_copy(
            air_hbm.at[i * chunk : (i + 1) * chunk],
            x0.at[i * chunk : (i + 1) * chunk, :, rim : rim + block],
            air_sem.at[i],
        )
        for i in range(parts)
    ]
    load_sea = pltpu.make_async_copy(sea_hbm, y0.at[:, :, orim : orim + cells], loc_sem.at[1])
    small = [
        pltpu.make_async_copy(src, dst, loc_sem.at[2 + i])
        for i, (src, dst) in enumerate((
            (weight_hbm, weight_ref), (anb_hbm, anb_ref), (adf_hbm, adf_ref),
            (send_hbm, send_ref), (onb_hbm, onb_ref), (odf_hbm, odf_ref), (vm_hbm, vm_ref),
            (slot_hbm, slot_ref), (rw_hbm, rw_ref),
        ))
    ]
    for copy in load_air:
        copy.start()
    for copy in small:
        copy.start()
    load_sea.start()
    for copy in small:
        copy.wait()

    def offsets(ref):
        places = ref[...]
        return (places - HALO - lane_of(places.shape)).astype(jnp.float32)

    own = slice(rim, rim + block)
    rbuf[0, 4 : 4 + nba, own] = adf_ref[...]
    rbuf[0, 8 : 8 + nba, own] = offsets(anb_ref)
    rbuf[0, 12:16, own] = jnp.zeros((4, block), jnp.float32)
    sea_own = slice(orim, orim + cells)
    qbuf[0:nbo, sea_own] = offsets(onb_ref)
    qbuf[6 : 6 + nbo, sea_own] = odf_ref[...]
    qbuf[12:13, sea_own] = vm_ref[...]
    qbuf[13 : 13 + krem, sea_own] = slot_ref[...].astype(jnp.float32)
    qbuf[17 : 17 + krem, sea_own] = rw_ref[...]
    qbuf[21:24, sea_own] = jnp.zeros((3, cells), jnp.float32)
    table[0] = jnp.broadcast_to(send_ref[...], table.shape[1:])

    mean = jnp.zeros((flds, block), jnp.float32)
    for i in range(parts):
        load_air[i].wait()
        for k in range(i * chunk, (i + 1) * chunk):
            mean = mean + weight_ref[k] * x0[k, :, own]
    rbuf[0, 0:flds, own] = mean
    load_sea.wait()

    pl.semaphore_wait(barrier, npos - 1 + 3 * (nlev - 1))

    def remote(src, dst, send, recv, device):
        return pltpu.make_async_remote_copy(
            src_ref=src, dst_ref=dst, send_sem=send, recv_sem=recv,
            device_id=device, device_id_type=MESH,
        )

    copies = []
    avg = []
    lefts = slice(0, rim)
    rights = slice(rim + block, rim + block + rim)
    low = slice(rim, 2 * rim)
    high = slice(block, block + rim)
    for j in range(nlev):
        rel = (nlev - j) % nlev
        rows = slice(0, 16) if j == 0 else slice(0, 8)
        for w, (src, dst, step) in enumerate(((high, lefts, 1), (own, own, 0), (low, rights, -1))):
            if j == 0 and step == 0:
                continue
            avg.append(
                remote(
                    rbuf.at[0, rows, src], rbuf.at[rel, rows, dst],
                    avg_send.at[rel * 3 + w], avg_recv.at[rel * 3 + w], at(d + step, l + j),
                )
            )
    tabs = [remote(table.at[0], table.at[1], tab_send.at[0], tab_recv.at[0], at(d, l + 1))]
    if nlev > 2:
        tabs.append(remote(table.at[0], table.at[2], tab_send.at[1], tab_recv.at[1], at(d, l - 1)))
    q_high, q_left = slice(cells, cells + orim), slice(0, orim)
    q_low, q_right = slice(orim, 2 * orim), slice(orim + cells, orim + cells + orim)
    qs = [
        remote(qbuf.at[:, q_high], qbuf.at[:, q_left], q_send.at[0], q_recv.at[0], sea_at(1)),
        remote(qbuf.at[:, q_low], qbuf.at[:, q_right], q_send.at[1], q_recv.at[1], sea_at(-1)),
    ]
    seas = [
        remote(y0.at[:, :, q_high], y0.at[:, :, q_left], sea_send.at[0], sea_recv.at[0], sea_at(1)),
        remote(y0.at[:, :, q_low], y0.at[:, :, q_right], sea_send.at[1], sea_recv.at[1], sea_at(-1)),
    ]
    airs = [
        remote(x0.at[:, :, high], x0.at[:, :, lefts], air_send.at[0], air_recv.at[0], at(d + 1, l)),
        remote(x0.at[:, :, low], x0.at[:, :, rights], air_send.at[1], air_recv.at[1], at(d - 1, l)),
    ]
    for copy in avg + tabs + qs + seas + airs:
        copy.start()

    def tables(data, shift):
        span = data.shape[1]
        moved = pltpu.roll(data, span - HALO, axis=1) if shift else data
        rates = moved[4 : 4 + nba]
        tile_lane = jnp.bitwise_and(lane_of((nba, span)), LANE - 1)
        places = moved[8 : 8 + nba].astype(jnp.int32) + tile_lane + HALO
        return places, rates, 1.0 - jnp.sum(rates, axis=0, keepdims=True)

    row_ids = lax.broadcasted_iota(jnp.int32, (2 * LANE, LANE), 0)
    self_ids = lane_of((2 * LANE, LANE)) + HALO

    def build(index, places, rates, keep, out=mats):
        matrix = jnp.where(row_ids == self_ids, keep, 0.0)
        for n in range(places.shape[0]):
            matrix = matrix + jnp.where(row_ids == places[n : n + 1], rates[n : n + 1], 0.0)
        upper = matrix.astype(jnp.bfloat16)
        out[index, :, 0:LANE] = upper
        out[index, :, LANE:] = (matrix - upper.astype(jnp.float32)).astype(jnp.bfloat16)

    def apply(x, matrix):
        count = x.shape[0]
        upper = x.astype(jnp.bfloat16)
        lower = (x - upper.astype(jnp.float32)).astype(jnp.bfloat16)
        both = jnp.concatenate([upper, lower], axis=0)
        prod = jnp.dot(both, matrix, preferred_element_type=jnp.float32)
        rest_sum = prod[count:, 0:LANE] + prod[:count, LANE:] + prod[count:, LANE:]
        return prod[:count, 0:LANE] + rest_sum

    def sea_tables(data, shift):
        span = data.shape[1]
        moved = pltpu.roll(data, span - HALO, axis=1) if shift else data
        rates = moved[6 : 6 + nbo]
        tile_lane = jnp.bitwise_and(lane_of((nbo, span)), LANE - 1)
        places = moved[0:nbo].astype(jnp.int32) + tile_lane + HALO
        return places, rates, 1.0 - jnp.sum(rates, axis=0, keepdims=True), moved[12:13]

    wide = rbuf.shape[2]
    own_data = rbuf[0, :, own]
    rim_tiles, block_tiles = rim // LANE, block // LANE
    shifted_count = wide // LANE - 1
    done = set()
    for shift in range(2):
        places, rates, keep = tables(own_data, shift)
        for t in range(block_tiles - shift):
            cols = slice(t * LANE, (t + 1) * LANE)
            index = rim_tiles + t + (0 if shift else shifted_count - 1)
            build(index, places[:, cols], rates[:, cols], keep[:, cols])
            done.add(index)

    def flatten(cols):
        for k in range(0, levs, 2):
            xf[4 * k : 4 * k + 8, cols] = jnp.concatenate([x0[k, :, cols], x0[k + 1, :, cols]], axis=0)

    flatten(own)

    sea_shifted = qbuf.shape[1] // LANE - 1
    sea_done = set()
    for shift in range(2):
        places, rates, keep, _ = sea_tables(qbuf[:, sea_own], shift)
        for t in range(cells // LANE - shift):
            cols = slice(t * LANE, (t + 1) * LANE)
            index = orim // LANE + t + (0 if shift else sea_shifted - 1)
            build(index, places[:, cols], rates[:, cols], keep[:, cols], sea_mats)
            sea_done.add(index)

    for copy in avg:
        copy.wait_recv()
    packed = rbuf[0]
    for shift in range(2):
        places, rates, keep = tables(packed, shift)
        aplace[shift, 0:nba] = places
        arate[shift, 0:nba] = rates
        arate[shift, nba : nba + 1] = keep

    def air_tile(k, t, first, second):
        shift, base = (1 - k % 2), (k + 1) // 2
        cols = slice((base + t) * LANE, (base + t + 1) * LANE)
        return mix_tile(
            first, second, aplace[shift, 0:nba, cols], arate[shift, 0:nba, cols],
            arate[shift, nba : nba + 1, cols],
        )

    total = rbuf[0, 0:8]
    for j in range(1, nlev):
        total = total + rbuf[j, 0:8]
    top = lax.broadcasted_iota(jnp.int32, (8, LANE), 0)
    tiles = []
    for t in range(wide // LANE):
        tile = total[:, t * LANE : (t + 1) * LANE]
        tiles.append(jnp.where(top < 4, tile, pltpu.roll(tile, 4, axis=0)))
    for k in range(STEPS_ATM):
        tiles = [air_tile(k, t, tiles[t], tiles[t + 1]) for t in range(len(tiles) - 1)]

    for copy in tabs:
        copy.wait_recv()
    lane8 = lane_of((8, LANE))
    per_tile = LANE // cap
    up_row = 2 if nlev > 2 else 1

    def request(pos):
        odd = lax.rem(pos, 2)
        forward = jnp.where(odd == 0, l > 0, l == nlev - 1)
        cross = lax.rem(pos + jnp.where(forward, 1, npos - 1), npos)
        start = pl.multiple_of(pos // per_tile * LANE, LANE)
        mine = table[0, :, pl.ds(start, LANE)]
        mine = pltpu.roll(mine, lax.rem(LANE - lax.rem(pos, per_tile) // 2 * 2 * cap, LANE), axis=1)
        start = pl.multiple_of(cross // per_tile * LANE, LANE)
        row = jnp.where(odd == 0, 1, up_row)
        other = table[row, :, pl.ds(start, LANE)]
        turn = lax.rem(2 * cap - lax.rem(cross, per_tile) * cap + LANE, LANE)
        other = pltpu.roll(other, turn, axis=1)
        column = jnp.where(lane8 < 2 * cap, mine, other)
        lanes = jnp.bitwise_and(column, LANE - 1)
        value = pick(tiles[0], lanes)
        for t in range(1, len(tiles)):
            value = jnp.where(column >= t * LANE, pick(tiles[t], lanes), value)
        return value

    routes = []
    for k in range(npos):
        pos = lax.rem(d + k, npos)
        if k == 0:
            pin[0] = request(pos)
            continue
        pout[k] = request(pos)
        copy = remote(pout.at[k], pin.at[k], route_send.at[k], route_recv.at[k], at(pos, l))
        copy.start()
        routes.append(copy)

    for copy in qs + seas:
        copy.wait_recv()
    qall = qbuf[...]
    qwide = qall.shape[1]
    for shift in range(2):
        places, rates, keep, mixing = sea_tables(qall, shift)
        oplace[shift, 0:nbo] = places
        orate[shift, 0:nbo] = rates
        orate[shift, nbo : nbo + 1] = keep
        orate[shift, nbo + 1 : nbo + 2] = mixing
        for t in range(1 - shift, sea_shifted):
            index = t + (0 if shift else sea_shifted - 1)
            if index in sea_done or (shift == 0 and t > cells // LANE):
                continue
            cols = slice(t * LANE, (t + 1) * LANE)
            build(index, places[:, cols], rates[:, cols], keep[:, cols], sea_mats)

    def sea_cols(k, t):
        base = (k + 1) // 2
        return 1 - k % 2, slice((base + t) * LANE, (base + t + 1) * LANE)

    def sea_tile(k, t, first, second):
        shift, cols = sea_cols(k, t)
        return mix_tile(
            first, second, oplace[shift, 0:nbo, cols], orate[shift, 0:nbo, cols],
            orate[shift, nbo : nbo + 1, cols],
        )

    def sea_vertical(k, t):
        shift, cols = sea_cols(k, t)
        return orate[shift, nbo + 1 : nbo + 2, cols]

    src = y0
    tracers, depth = y0.shape[0], y0.shape[1]
    level = lax.broadcasted_iota(jnp.int32, (depth, LANE), 0)
    for k in range(STEPS_OCN):
        dst = sea_out if k == STEPS_OCN - 1 else ya
        for t in range(dst.shape[2] // LANE):
            shift, base = 1 - k % 2, (k + 1) // 2
            index = base + t + (0 if shift else sea_shifted - 1)
            x = src[:, :, t * LANE : (t + 2) * LANE].reshape(tracers * depth, 2 * LANE)
            mixed = apply(x, sea_mats[index])
            for tracer in range(tracers):
                v = mixed[tracer * depth : (tracer + 1) * depth]
                up = jnp.where(level == 0, v, pltpu.roll(v, 1, axis=0))
                down = jnp.where(level == depth - 1, v, pltpu.roll(v, depth - 1, axis=0))
                v = v + sea_vertical(k, t) * (up - 2.0 * v + down)
                dst[tracer, :, t * LANE : (t + 1) * LANE] = v
        src = dst

    for shift in range(2):
        for t in range(1 - shift, shifted_count):
            index = t + (0 if shift else shifted_count - 1)
            if index in done:
                continue
            cols = slice(t * LANE, (t + 1) * LANE)
            build(
                index, aplace[shift, 0:nba, cols], arate[shift, 0:nba, cols],
                arate[shift, nba : nba + 1, cols],
            )
    for copy in airs:
        copy.wait_recv()
    flatten(lefts)
    flatten(rights)
    src = xf
    for k in range(STEPS_ATM):
        dst = xa if k % 2 == 0 else xb
        for t in range(shifted_count - k):
            shift, base = 1 - k % 2, (k + 1) // 2
            index = base + t + (0 if shift else shifted_count - 1)
            x = src[:, t * LANE : (t + 2) * LANE]
            result = apply(x, mats[index])
            cols = slice(t * LANE, (t + 1) * LANE)
            if k < STEPS_ATM - 1:
                dst[:, cols] = result
            else:
                for level in range(levs):
                    air_out[level, :, cols] = result[4 * level : 4 * level + 4]
        src = dst
    save_air = [
        pltpu.make_async_copy(
            air_out.at[i * chunk : (i + 1) * chunk],
            air_res.at[i * chunk : (i + 1) * chunk],
            out_sem.at[i],
        )
        for i in range(parts)
    ]
    for copy in save_air:
        copy.start()

    sub8 = lax.broadcasted_iota(jnp.int32, (8, LANE), 0)
    kinds = [jnp.where(s == 0, 2, 0)] + [s] * (cells // LANE) + [jnp.where(s == 0, 1, 2)]
    bits = cap.bit_length() - 1
    ready = []
    for t in range(qwide // LANE):
        cols = slice(t * LANE, (t + 1) * LANE)
        slots = qbuf[13 : 13 + krem, cols].astype(jnp.int32)
        weights = qbuf[17 : 17 + krem, cols]
        weights = weights / jnp.sum(weights, axis=0, keepdims=True)
        terms = []
        for m in range(krem // 2):
            m2 = m + krem // 2
            slot = jnp.where(sub8 < 4, slots[m : m + 1], slots[m2 : m2 + 1])
            weight2 = jnp.where(sub8 < 4, weights[m : m + 1], weights[m2 : m2 + 1])
            far = d - lax.shift_right_logical(slot, bits)
            far = jnp.where(far < 0, far + npos, far)
            terms.append((far, jnp.bitwise_and(slot, cap - 1) + kinds[t] * cap, weight2))
        sst = y0[0, 0:1, cols]
        ready.append((terms, sst, 0.5 * jnp.exp(0.25 * sst), 1.0 + 0.2 * y0[1, 0:1, cols]))
    for copy in routes:
        copy.wait_recv()
    changes = []
    for terms, sst, humid_sea, brine_rate in ready:
        acc = jnp.zeros((8, LANE), jnp.float32)
        for far, lanes, weight2 in terms:
            value = pick(pin[0], lanes)
            for k in range(1, npos):
                value = jnp.where(far == k, pick(pin[k], lanes), value)
            acc = acc + weight2 * value
        acc = acc + pltpu.roll(acc, 4, axis=0)
        temp, humid, east, north = (acc[i : i + 1] for i in range(4))
        wind = jnp.sqrt(east * east + north * north + 1.0)
        evap = 0.2 * wind * (humid_sea - humid)
        heat = 0.3 * wind * (temp - sst) - 1.5 * evap
        brine = 0.5 * evap * brine_rate
        changes.append(jnp.where(sub8 == 0, heat, jnp.where(sub8 == 1, brine, 0.0)))
    later = []
    for t in range(len(changes) - 1):
        v = sea_tile(0, t, changes[t], changes[t + 1])
        mixing = sea_vertical(0, t)
        later.append(jnp.where(sub8 < 2, (1.0 - mixing) * v, mixing * pltpu.roll(v, 2, axis=0)))
    for t in range(len(later) - 1):
        v = sea_tile(1, t, later[t], later[t + 1])
        mixing = sea_vertical(1, t)
        cols = slice(t * LANE, (t + 1) * LANE)
        for tracer in range(2):
            a, b = v[tracer : tracer + 1], v[2 + tracer : 3 + tracer]
            sea_out[tracer, 0:1, cols] += a + mixing * (b - a)
            sea_out[tracer, 1:2, cols] += b + mixing * (a - 2.0 * b)
            sea_out[tracer, 2:3, cols] += mixing * b

    save_sea = pltpu.make_async_copy(sea_out, sea_res, loc_sem.at[0])
    save_sea.start()
    for copy in avg + tabs + qs + seas + airs + routes:
        copy.wait_send()
    for copy in save_air + [save_sea]:
        copy.wait()


def body(
    npos,
    nlev,
    atmos_state,
    ocean_state,
    level_weight,
    atmos_neighbors,
    atmos_diffusion,
    ocean_neighbors,
    ocean_diffusion,
    vertical_mixing,
    send_columns,
    read_slots,
    remap_weight,
):
    flds, levs, block = atmos_state.shape
    tracers, depth, cells = ocean_state.shape
    wide = block + 2 * STEPS_ATM * HALO
    qwide = cells + 2 * STEPS_OCN * HALO
    rows = -(-flds * levs // 16) * 16
    vmem = pl.BlockSpec(memory_space=pltpu.VMEM)
    hbm = pl.BlockSpec(memory_space=pltpu.HBM)
    dma = pltpu.SemaphoreType.DMA
    f32, i32 = jnp.float32, jnp.int32
    places = send_columns.shape[0]
    small = (
        (atmos_neighbors.shape, i32),
        (atmos_diffusion.shape, f32),
        (ocean_neighbors.shape, i32),
        (ocean_diffusion.shape, f32),
        ((1, cells), f32),
        ((1, places), i32),
        (read_slots.shape, i32),
        (remap_weight.shape, f32),
    )
    air, sea = pl.pallas_call(
        functools.partial(kernel, npos, nlev),
        out_shape=(
            jax.ShapeDtypeStruct((levs, flds, block), f32),
            jax.ShapeDtypeStruct(ocean_state.shape, f32),
        ),
        in_specs=[hbm] * 11,
        out_specs=(hbm, hbm),
        scratch_shapes=[
            pltpu.VMEM((levs, flds, block), f32),
            pltpu.VMEM(ocean_state.shape, f32),
            pltpu.SMEM(level_weight.shape, f32),
            *(pltpu.VMEM(shape, kind) for shape, kind in small),
            pltpu.VMEM((levs, flds, wide), f32),
            pltpu.VMEM((rows, wide), f32),
            pltpu.VMEM((rows, wide - LANE), f32),
            pltpu.VMEM((rows, wide - 2 * LANE), f32),
            pltpu.VMEM((2 * wide // LANE - 3, 2 * LANE, 2 * LANE), jnp.bfloat16),
            pltpu.VMEM((2 * qwide // LANE - 3, 2 * LANE, 2 * LANE), jnp.bfloat16),
            pltpu.VMEM((tracers, depth, qwide), f32),
            pltpu.VMEM((tracers, depth, qwide - LANE), f32),
            pltpu.VMEM((nlev, 16, wide), f32),
            pltpu.VMEM((24, qwide), f32),
            pltpu.VMEM((2, 8, wide), i32),
            pltpu.VMEM((2, 8, wide), f32),
            pltpu.VMEM((2, 8, qwide), i32),
            pltpu.VMEM((2, 8, qwide), f32),
            pltpu.VMEM((3, 8, places), i32),
            pltpu.VMEM((npos, 8, LANE), f32),
            pltpu.VMEM((npos, 8, LANE), f32),
            dma((11,)),
            dma((parts_of(levs),)),
            dma((parts_of(levs),)),
            dma((3 * nlev,)),
            dma((3 * nlev,)),
            *(dma((2,)) for _ in range(8)),
            dma((npos,)),
            dma((npos,)),
        ],
        compiler_params=pltpu.CompilerParams(
            collective_id=0, has_side_effects=True, vmem_limit_bytes=60 * 1024 * 1024
        ),
    )(
        jnp.transpose(atmos_state, (1, 0, 2)),
        ocean_state,
        level_weight,
        atmos_neighbors,
        atmos_diffusion,
        ocean_neighbors,
        ocean_diffusion,
        vertical_mixing[None, :],
        send_columns[None, :],
        read_slots,
        remap_weight,
    )
    air, sea = pl.pallas_call(
        move_out,
        out_shape=(
            jax.ShapeDtypeStruct((levs, flds, block), f32),
            jax.ShapeDtypeStruct(ocean_state.shape, f32),
        ),
        in_specs=[vmem] * 2,
        out_specs=(hbm, hbm),
        scratch_shapes=[dma((parts_of(levs),)), dma((2,))],
    )(air, sea)
    return jnp.transpose(air, (1, 0, 2)), sea


def parts_of(levs):
    return next(n for n in (6, 4, 3, 2, 1) if levs % n == 0)


def move_out(air, sea, air_out, sea_out, sems, sea_sems):
    parts = parts_of(air.shape[0])
    chunk = air.shape[0] // parts
    copies = [
        pltpu.make_async_copy(
            air.at[i * chunk : (i + 1) * chunk],
            air_out.at[i * chunk : (i + 1) * chunk],
            sems.at[i],
        )
        for i in range(parts)
    ]
    copies += [pltpu.make_async_copy(sea.at[i], sea_out.at[i], sea_sems.at[i]) for i in range(2)]
    for copy in copies:
        copy.start()
    for copy in copies:
        copy.wait()


def solution(mesh):
    npos = mesh.shape["comp"] * mesh.shape["sub"]
    nlev = mesh.shape["lev"]
    in_specs = (
        P(None, "lev", ("member", "comp", "sub")),
        P(None, None, ("member", "comp", "lev", "sub")),
        P("lev"),
        P(None, ("comp", "sub")),
        P(None, ("comp", "sub")),
        P(None, ("comp", "lev", "sub")),
        P(None, ("comp", "lev", "sub")),
        P(("comp", "lev", "sub")),
        P(("comp", "lev", "sub")),
        P(None, ("comp", "lev", "sub")),
        P(None, ("comp", "lev", "sub")),
    )
    out_specs = (
        P(None, "lev", ("member", "comp", "sub")),
        P(None, None, ("member", "comp", "lev", "sub")),
    )
    return jax.shard_map(
        functools.partial(body, npos, nlev),
        mesh=mesh,
        in_specs=in_specs,
        out_specs=out_specs,
        check_vma=False,
    )
```
